32 devices in a mesh: groups: 2 (over y), fsdp: 4 (over z), tensor: 2 (over core), adapter: 2 (over x).
Axes of the slice: x: 2, y: 2, z: 4, core: 2. Of those that a mesh axis runs over, the one named last changes fastest.
Arguments:
- acts: bfloat16 [8192, 5120], P(('groups', 'fsdp'), ('adapter', 'tensor')), parts along dimension 0, may hold values from -6 to 6
- cotangent: bfloat16 [8192, 2, 1024], P(('groups', 'fsdp', 'adapter'), None, 'tensor'), parts along dimension 0, may hold values from -1.5 to 1.5
- key_value_weight: bfloat16 [5120, 2, 1024], P(('adapter', 'fsdp'), None, 'tensor'), may hold values from -0.078125 to 0.078125
- adapter_first_factor: bfloat16 [96, 2, 327680], P(None, None, ('adapter', 'tensor', 'fsdp')), may hold values from -0.078125 to 0.078125
- adapter_second_factor: bfloat16 [96, 2, 64, 1024], P(None, None, 'fsdp', 'tensor'), may hold values from -0.75 to 0.75
- adapter_of_block: int32 [32], P('groups'), parts along dimension 0, may hold values from 0 to 95
- occupied_rows: int32 [32], P('groups'), parts along dimension 0, may hold values from 32 to 256, as said below
Outputs:
- input_gradient: bfloat16 [8192, 5120], P(('groups', 'fsdp'), ('adapter', 'tensor')), parts along dimension 0
- down_grad: bfloat16 [192, 2, 327680], P('groups', None, ('adapter', 'tensor', 'fsdp')), parts along dimension 0
- up_grad: bfloat16 [192, 2, 64, 1024], P('groups', None, 'fsdp', 'tensor'), parts along dimension 0
The draws below stay inside these ranges and needn't reach their ends.
There are 2 independent parts, one for each index of `groups`. The reference program is written for one: setup_inputs(seed, part) draws one part's arguments, and reference() takes and returns one part's arrays. A program takes and returns all parts, laid end to end along the dimension named above; an argument that names none is the same for every part. Nothing has to cross between parts.
Inputs may be any that keep to these rules, and one draw needn't show every extreme that they name: The first occupied_rows rows of a block hold tokens, the rest is padding; in every draw some block is full.
All inputs are finite; a program needn't handle non-finite values.
Results may differ from the reference program's by a relative error of at most 0.014.
Values may be sent and summed in bfloat16 or wider, within the bound.
A program may use at most 128 MiB of HBM per device.

```python
import math
import jax
import jax.numpy as jnp
import numpy as np
from jax import lax

MODEL_WIDTH = 5120
KEY_VALUE_WIDTH = 1024
ADAPTER_TOTAL = 96
ADAPTER_RANK = 64
BLOCK = 256
BLK_DEV = 4
ROWS = 4096
BLOCKS = 16
N_FSDP = 4
N_TENSOR = 2


def draw_occupied_rows(key, part):
    key = jax.random.fold_in(key, 7)
    first_key, second_key = jax.random.split(key)
    lengths = jax.random.randint(first_key, (BLOCKS,), BLOCK // 8, BLOCK + 1)
    chosen = jax.random.randint(second_key, (), 0, BLOCKS)
    return jnp.where(jnp.arange(BLOCKS) == chosen, BLOCK, lengths).astype(jnp.int32)


def place_ends(entries, rng, smallest, largest):
    longest = entries.shape.index(max(entries.shape))
    spots = []
    for shift in (0, 1):
        where = [jax.random.randint(jax.random.fold_in(rng, axis), (), 0, length) for axis, length in enumerate(entries.shape)]
        where[longest] = (where[longest] + shift) % entries.shape[longest]
        spots.append(tuple(where))
    return entries.at[spots[0]].set(smallest).at[spots[1]].set(largest)


def block_scale(rng, shape, cuts, least, high):
    loudness, own = 1.0, jax.random.fold_in(rng, 6)
    for position, blocks in cuts:
        steps = jnp.exp(jax.random.uniform(jax.random.fold_in(own, position), (blocks,), jnp.float32, least / len(cuts), high / len(cuts)))
        loudness = loudness * jnp.repeat(steps, shape[position] // blocks).reshape([-1 if axis == position else 1 for axis in range(len(shape))])
    return loudness


def cumulative_ranks(number_of, lean):
    portions = [(1 << 20) // math.isqrt(standing ** lean) + 1 for standing in range(1, number_of + 1)]
    scale = 1 + sum(portions) // (1 << 30)
    return np.cumsum(np.array([max(1, weight // scale) for weight in portions]))


def skewed_ids(rng, dims, amount, lean):
    listing = cumulative_ranks(amount, lean)
    ticket = jax.random.randint(jax.random.fold_in(rng, 1), dims, 0, int(listing[amount - 1]))
    grade = jnp.searchsorted(jnp.asarray(listing, jnp.int32), ticket, side="right")
    return jax.random.permutation(jax.random.fold_in(rng, 2), amount)[grade].astype(jnp.int32)


def gaussian(key, extent, width, bound, pieces=(), kind=jnp.bfloat16):
    result = width * jax.random.normal(key, extent, jnp.float32)
    if pieces:
        result = result * block_scale(key, extent, pieces, -0.22, 0.18)
    return jnp.clip(result, -bound, bound).astype(kind)


def setup_inputs(seed: int = 0, part: int = 0) -> dict:
    seeds = jax.random.split(jax.random.key(seed), 8)
    part_splits = jax.random.split(jax.random.fold_in(seeds[7], part), 8)
    return {
        "acts": gaussian(part_splits[0], (ROWS, MODEL_WIDTH), 1.0, 6.0, ((0, 4), (1, 4))),
        "cotangent": gaussian(part_splits[1], (ROWS, 2, KEY_VALUE_WIDTH), 0.25, 1.5, ((0, 8), (2, 2))),
        "key_value_weight": gaussian(seeds[2], (MODEL_WIDTH, 2, KEY_VALUE_WIDTH), MODEL_WIDTH ** -0.5, 0.078125, ((0, 8), (2, 2))),
        "adapter_first_factor": gaussian(seeds[3], (ADAPTER_TOTAL, 2, MODEL_WIDTH * ADAPTER_RANK), MODEL_WIDTH ** -0.5, 0.078125, ((2, 16),)),
        "adapter_second_factor": gaussian(seeds[4], (ADAPTER_TOTAL, 2, ADAPTER_RANK, KEY_VALUE_WIDTH), ADAPTER_RANK ** -0.5, 0.75, ((2, 4), (3, 2))),
        "adapter_of_block": place_ends(skewed_ids(part_splits[5], (BLOCKS,), ADAPTER_TOTAL, 2), jax.random.fold_in(part_splits[5], 3), 0, ADAPTER_TOTAL - 1).astype(jnp.int32),
        "occupied_rows": draw_occupied_rows(jax.random.fold_in(jax.random.fold_in(seeds[7], part), 71), part),
    }


adapter_scale = 2.0


def reference(acts, cotangent, key_value_weight, adapter_first_factor, adapter_second_factor, adapter_of_block, occupied_rows):
    head_half = KEY_VALUE_WIDTH // N_TENSOR
    rows_in_group = BLK_DEV * BLOCK
    positions = jnp.arange(ROWS, dtype=jnp.int32)
    limits = jnp.repeat(occupied_rows, BLOCK, total_repeat_length=ROWS)
    kept_rows = (positions % BLOCK) < limits
    masked = jnp.where(kept_rows[:, None, None], cotangent, jnp.zeros_like(cotangent))
    down_factor_table = adapter_first_factor.reshape(ADAPTER_TOTAL, 2, MODEL_WIDTH, ADAPTER_RANK)

    def per_group(totals, group_index):
        grad_down, grad_up = totals
        start = (group_index * rows_in_group).astype(jnp.int32)
        acts_group = lax.dynamic_slice_in_dim(acts, start, rows_in_group, 0)
        cot_group = lax.dynamic_slice_in_dim(masked, start, rows_in_group, 0)
        block_indices = lax.dynamic_slice_in_dim(adapter_of_block, (group_index * BLK_DEV).astype(jnp.int32), BLK_DEV, 0)
        frozen_path_gradient = jnp.zeros((rows_in_group, MODEL_WIDTH), jnp.float32)
        for which in range(N_TENSOR):
            cot_part = cot_group[:, :, which * head_half:(which + 1) * head_half].reshape(rows_in_group, 2 * head_half)
            weight_part = key_value_weight[:, :, which * head_half:(which + 1) * head_half].reshape(MODEL_WIDTH, 2 * head_half)
            partial_value = jnp.dot(cot_part, weight_part.T, preferred_element_type=jnp.float32).astype(jnp.bfloat16)
            frozen_path_gradient = frozen_path_gradient + partial_value.astype(jnp.float32)
        adapter_down_factor = down_factor_table[block_indices].astype(jnp.float32)
        adapter_up_factor = adapter_second_factor[block_indices].astype(jnp.float32)
        cotangent_blocks = cot_group.reshape(BLK_DEV, BLOCK, 2, KEY_VALUE_WIDTH).astype(jnp.float32)
        activation_blocks = acts_group.reshape(BLK_DEV, BLOCK, MODEL_WIDTH).astype(jnp.float32)
        head_gradient = jnp.einsum("bnch,bcrh->bncr", cotangent_blocks, adapter_up_factor)
        head_gradient = lax.optimization_barrier(head_gradient.astype(jnp.bfloat16)).astype(jnp.float32)
        reduced_activations = jnp.einsum("bnd,bcdr->bncr", activation_blocks, adapter_down_factor)
        reduced_activations = lax.optimization_barrier(reduced_activations.astype(jnp.bfloat16)).astype(jnp.float32)
        adapter_term = adapter_scale * jnp.einsum("oyet,oemt->oym", head_gradient, adapter_down_factor).reshape(rows_in_group, MODEL_WIDTH)
        input_portion = (frozen_path_gradient + adapter_term).astype(jnp.bfloat16)
        block_down_factor = adapter_scale * jnp.einsum("mky,mkzl->mzyl", activation_blocks, head_gradient)
        block_up_factor = adapter_scale * jnp.einsum("ijfm,ijfy->ifmy", reduced_activations, cotangent_blocks)
        grad_down = grad_down.at[block_indices].add(block_down_factor)
        grad_up = grad_up.at[block_indices].add(block_up_factor)
        return (grad_down, grad_up), input_portion

    start_tables = (jnp.zeros((ADAPTER_TOTAL, 2, MODEL_WIDTH, ADAPTER_RANK), jnp.float32), jnp.zeros((ADAPTER_TOTAL, 2, ADAPTER_RANK, KEY_VALUE_WIDTH), jnp.float32))
    (grad_down, grad_up), input_parts = lax.scan(per_group, start_tables, jnp.arange(N_FSDP, dtype=jnp.int32))
    input_gradient = input_parts.reshape(ROWS, MODEL_WIDTH)
    return (input_gradient, grad_down.reshape(ADAPTER_TOTAL, 2, MODEL_WIDTH * ADAPTER_RANK).astype(jnp.bfloat16), grad_up.astype(jnp.bfloat16))
```

```python
import jax
import jax.numpy as jnp
from jax import lax
from jax.experimental import pallas as pl
from jax.experimental.pallas import tpu as pltpu
from jax.sharding import PartitionSpec as P

ADAPTER_TOTAL = 96
ADAPTER_RANK = 64
BLOCK = 256


adapter_scale = 2.0


def general_on_device(
    acts,
    cotangent,
    key_value_weight,
    adapter_first_factor,
    adapter_second_factor,
    adapter_of_block,
    occupied_rows,
):
    fsdp_count = lax.axis_size("fsdp")
    fsdp_index = lax.axis_index("fsdp")
    adapter_index = lax.axis_index("adapter")
    count_of_rows = acts.shape[0]
    feature_columns = acts.shape[1]
    block_count = count_of_rows // BLOCK
    quarter_rows = cotangent.shape[0]
    head_half = cotangent.shape[2]
    portion_length = adapter_first_factor.shape[2]
    rank_portion = adapter_second_factor.shape[2]
    live_mine = lax.dynamic_slice_in_dim(occupied_rows, fsdp_index * block_count, block_count, 0)
    limits = jnp.repeat(live_mine, BLOCK, total_repeat_length=count_of_rows)
    limit_quarter = lax.dynamic_slice_in_dim(limits, adapter_index * quarter_rows, quarter_rows, 0)
    offsets = adapter_index * quarter_rows + jnp.arange(quarter_rows, dtype=jnp.int32)
    kept_rows = offsets % BLOCK < limit_quarter
    masked = jnp.where(kept_rows[:, None, None], cotangent, jnp.zeros_like(cotangent))
    cot_full = lax.all_gather(masked, "adapter", axis=0, tiled=True)
    departing_down = jnp.take(adapter_first_factor, adapter_of_block, axis=0)
    departing_up = jnp.take(adapter_second_factor, adapter_of_block, axis=0)
    fetched_down, fetched_up = (
        lax.all_to_all(departing_down, "fsdp", split_axis=0, concat_axis=0, tiled=True),
        lax.all_to_all(departing_up, "fsdp", split_axis=0, concat_axis=0, tiled=True),
    )
    own_down = fetched_down.reshape(fsdp_count, block_count, 2, portion_length).transpose(
        1, 2, 0, 3
    )
    own_down = own_down.reshape(block_count, 2, feature_columns, ADAPTER_RANK)
    own_up = fetched_up.reshape(fsdp_count, block_count, 2, rank_portion, head_half).transpose(
        1, 2, 0, 3, 4
    )
    own_up = own_up.reshape(block_count, 2, ADAPTER_RANK, head_half)
    cotangent_blocks = cot_full.reshape(block_count, BLOCK, 2, head_half)
    activation_blocks = acts.reshape(block_count, BLOCK, feature_columns)
    feature_part = jnp.einsum(
        "bnd,bcdr->bncr", activation_blocks, own_down, preferred_element_type=jnp.float32
    )
    head_part = jnp.einsum(
        "bnch,bcrh->bncr", cotangent_blocks, own_up, preferred_element_type=jnp.float32
    )
    head_total = lax.psum(head_part.astype(jnp.bfloat16), "tensor")
    feature_total = lax.psum(feature_part.astype(jnp.bfloat16), ("tensor", "adapter"))
    adapter_term = adapter_scale * jnp.einsum(
        "oyet,oemt->oym", head_total, own_down, preferred_element_type=jnp.float32
    )
    adapter_term = adapter_term.reshape(count_of_rows, feature_columns)
    block_down_factor = adapter_scale * jnp.einsum(
        "mky,mkzl->mzyl", activation_blocks, head_total, preferred_element_type=jnp.float32
    )
    block_up_factor = adapter_scale * jnp.einsum(
        "ijfm,ijfy->ifmy", feature_total, cotangent_blocks, preferred_element_type=jnp.float32
    )
    partial_value = jnp.einsum(
        "nch,dch->nd",
        cot_full,
        lax.all_gather(key_value_weight, "fsdp", axis=0, tiled=True),
        preferred_element_type=jnp.float32,
    )
    frozen_path_gradient = lax.psum_scatter(
        partial_value.astype(jnp.bfloat16), "tensor", scatter_dimension=1, tiled=True
    ).astype(jnp.float32)
    input_gradient = (frozen_path_gradient + adapter_term).astype(jnp.bfloat16)
    send_down = block_down_factor.reshape(block_count, 2, fsdp_count, portion_length).transpose(
        2, 0, 1, 3
    )
    send_down = send_down.reshape(fsdp_count * block_count, 2, portion_length)
    send_up = block_up_factor.reshape(
        block_count, 2, fsdp_count, rank_portion, head_half
    ).transpose(2, 0, 1, 3, 4)
    send_up = send_up.reshape(fsdp_count * block_count, 2, rank_portion, head_half)
    back_down, back_up = (
        lax.all_to_all(
            send_down.astype(jnp.bfloat16), "fsdp", split_axis=0, concat_axis=0, tiled=True
        ).astype(send_down.dtype),
        lax.all_to_all(
            send_up.astype(jnp.bfloat16), "fsdp", split_axis=0, concat_axis=0, tiled=True
        ).astype(send_up.dtype),
    )
    selector = (
        adapter_of_block[None, :] == jnp.arange(ADAPTER_TOTAL, dtype=jnp.int32)[:, None]
    ).astype(jnp.float32)
    down_factor_table = jnp.dot(
        selector, back_down.reshape(back_down.shape[0], -1), precision=lax.Precision.HIGHEST
    )
    table_up = jnp.dot(
        selector, back_up.reshape(back_up.shape[0], -1), precision=lax.Precision.HIGHEST
    )
    down_grad = down_factor_table.reshape(ADAPTER_TOTAL, 2, portion_length).astype(jnp.bfloat16)
    up_grad = table_up.reshape(ADAPTER_TOTAL, 2, rank_portion, head_half).astype(jnp.bfloat16)
    return (input_gradient, down_grad, up_grad)


MESH = pl.DeviceIdType.MESH
F32 = jnp.float32
BF16 = jnp.bfloat16


def product(left, right, left_dim, right_dim):
    return lax.dot_general(
        left, right, (((left_dim,), (right_dim,)), ((), ())), preferred_element_type=F32
    )


def trade_pairs(table):
    rows = table.shape[0]
    groups = table.reshape(rows // 8, 8, 128)
    row_odd = lax.broadcasted_iota(jnp.int32, groups.shape, 1) % 2
    lane_high = lax.broadcasted_iota(jnp.int32, groups.shape, 2) // 64
    other = jnp.where(row_odd == 0, pltpu.roll(groups, 7, 1), pltpu.roll(groups, 1, 1))
    other = pltpu.roll(other, 64, 2)
    return jnp.where(row_odd == lane_high, groups, other).reshape(rows, 128)


def pick_kernel(ids_ref, first_ref, second_ref, first_out, second_out, first_sem, second_sem):
    copies = []
    for block in range(first_out.shape[0]):
        which = ids_ref[block]
        copies.append(
            pltpu.make_async_copy(second_ref.at[which], second_out.at[block], second_sem.at[block])
        )
        copies.append(
            pltpu.make_async_copy(first_ref.at[which], first_out.at[block], first_sem.at[block])
        )
    for copy in copies:
        copy.start()
    for copy in copies:
        copy.wait()


def table_kernel(
    ids_ref, down_ref, up_ref, down_out, up_out,
    zero_down, zero_up, sum_down, sum_up, total_down, total_up, first, zero_sem, row_sem,
):
    blocks = down_ref.shape[0]
    span = zero_down.shape[0]
    steps = down_out.shape[0] // span
    zero_down[...] = jnp.zeros_like(zero_down)
    zero_up[...] = jnp.zeros_like(zero_up)
    copies = []
    for step in range(steps):
        rows = pl.ds(step * span, span)
        copies.append(pltpu.make_async_copy(zero_down, down_out.at[rows], zero_sem.at[0, step]))
        copies.append(pltpu.make_async_copy(zero_up, up_out.at[rows], zero_sem.at[1, step]))
    for copy in copies:
        copy.start()

    def add_up(block, carry):
        mine = ids_ref[block]
        before = lax.fori_loop(
            0, block, lambda i, n: n + (ids_ref[i] == mine).astype(jnp.int32), jnp.int32(0)
        )
        first[block] = before

        @pl.when(before == 0)
        def _():
            total_down[...] = down_ref[block].astype(F32)
            total_up[...] = up_ref[:, block].astype(F32)

            def later(i, c):
                @pl.when(ids_ref[i] == mine)
                def _():
                    total_down[...] += down_ref[i].astype(F32)
                    total_up[...] += up_ref[:, i].astype(F32)
                return c

            lax.fori_loop(block + 1, blocks, later, 0)
            sum_down[block] = total_down[...].astype(BF16)
            sum_up[block] = total_up[...].astype(BF16)
        return carry

    lax.fori_loop(0, blocks, add_up, 0)
    for copy in copies:
        copy.wait()

    def rows_of(block):
        which = ids_ref[block]
        return (
            pltpu.make_async_copy(sum_down.at[block], down_out.at[which], row_sem.at[0, block]),
            pltpu.make_async_copy(sum_up.at[block], up_out.at[which], row_sem.at[1, block]),
        )

    def send(block, carry):
        @pl.when(first[block] == 0)
        def _():
            for copy in rows_of(block):
                copy.start()
        return carry

    def settle(block, carry):
        @pl.when(first[block] == 0)
        def _():
            for copy in rows_of(block):
                copy.wait()
        return carry

    lax.fori_loop(0, blocks, send, 0)
    lax.fori_loop(0, blocks, settle, 0)


def layer_kernel(
    cot_ref, w_ref, first_ref, second_ref, acts_ref,
    ig_ref, down_ref, up_ref,
    cot, weight, first, first_rows, second, acts,
    head_part, head_got, head, low_part, low_got, low_sum, low,
    down_stage, up_stage, part, part_got,
    local_sem, b_send, b_recv, a_send, a_recv, d_send, d_recv, u_send, u_recv,
    c_send, c_recv, h_send, h_recv, l_send, l_recv,
    w_send, w_recv, y_send, y_recv, p_send, p_recv, x_send, x_recv,
):
    f = lax.axis_index("fsdp")
    g = lax.axis_index("groups")
    t = lax.axis_index("tensor")
    a = lax.axis_index("adapter")
    other_g, other_t, other_a = 1 - g, 1 - t, 1 - a
    near = f + 1 - 2 * (f % 2)
    peers = (near, 2 - f // 2, 3 - 3 * (f // 2))
    inner = f * (3 - f) > 0
    blocks = 4
    portion = first_ref.shape[1]
    ranks = second_ref.shape[2]
    quarter = cot_ref.shape[1]
    half_rows = w_ref.shape[1] // 2
    pending = []

    def remote(source, target, send_sem, recv_sem, **where):
        return pltpu.make_async_remote_copy(
            src_ref=source, dst_ref=target, send_sem=send_sem, recv_sem=recv_sem,
            device_id=where, device_id_type=MESH,
        )

    def go(copy):
        copy.start()
        pending.append(copy)

    barrier = pltpu.get_barrier_semaphore()
    for where in (
        {"fsdp": peers[0]}, {"fsdp": peers[1]}, {"fsdp": peers[2]},
        {"groups": other_g}, {"tensor": other_t}, {"adapter": other_a},
    ):
        pl.semaphore_signal(barrier, inc=1, device_id=where, device_id_type=MESH)

    my_blocks = pl.ds(f * blocks, blocks)
    my_ranks = pl.ds(pl.multiple_of(f * ranks, 16), ranks)
    my_quarter = pl.ds(pl.multiple_of(a * quarter, 256), quarter)
    other_quarter = pl.ds(pl.multiple_of(other_a * quarter, 256), quarter)
    own = [
        pltpu.make_async_copy(second_ref.at[my_blocks, a], second.at[:, my_ranks], local_sem.at[0]),
        pltpu.make_async_copy(cot_ref, cot.at[:, my_quarter], local_sem.at[1]),
        pltpu.make_async_copy(acts_ref, acts, local_sem.at[2]),
        pltpu.make_async_copy(w_ref, weight.at[f], local_sem.at[3]),
        pltpu.make_async_copy(first_ref.at[my_blocks], first.at[f], local_sem.at[4]),
    ]
    for copy in own:
        copy.start()
    pl.semaphore_wait(barrier, 6)

    for i, peer in enumerate(peers):
        go(remote(
            second_ref.at[pl.ds(peer * blocks, blocks), a], second.at[:, my_ranks],
            b_send.at[i], b_recv.at[f], fsdp=peer,
        ))
    for c in (other_a, a):
        go(remote(
            cot_ref.at[c], cot.at[c, my_quarter], c_send.at[c], c_recv.at[c], adapter=other_a
        ))
    for i, peer in enumerate(peers):
        go(remote(
            first_ref.at[pl.ds(peer * blocks, blocks)], first.at[f],
            a_send.at[i], a_recv.at[f], fsdp=peer,
        ))

    def piece(s, c, sub):
        return weight.at[s, c, pl.ds(sub * half_rows, half_rows)]

    def weight_copy(s, sub, slot, target):
        return remote(
            piece(s, g, sub), piece(s, g, sub), w_send.at[slot, sub], w_recv.at[s, sub], fsdp=target
        )

    def twin_copy(s, c, j, sub):
        return remote(
            piece(s, c, sub), piece(s, c, sub), y_send.at[j, sub], y_recv.at[s, sub], groups=other_g
        )

    onward = (3 - f, (f - 1) * 3, (f - 1) * 3)

    def pass_on(j):
        s = peers[j]
        for sub in range(2):
            weight_copy(s, sub, 0, near).wait_recv()

            @pl.when(inner)
            def _():
                weight_copy(s, sub, 2 + j, onward[j]).start()

            go(twin_copy(s, g, j, sub))

    own[3].wait()
    for sub in range(2):
        go(weight_copy(f, sub, 0, near))

        @pl.when(inner)
        def _():
            weight_copy(f, sub, 1, 3 - f).start()

    own[0].wait()
    own[1].wait()
    for i, peer in enumerate(peers):
        remote(
            second_ref.at[pl.ds(peer * blocks, blocks), a],
            second.at[:, pl.ds(pl.multiple_of(peer * ranks, 16), ranks)],
            b_send.at[i], b_recv.at[peer], fsdp=peer,
        ).wait_recv()

    def cot_arrival(c):
        remote(
            cot_ref.at[c], cot.at[c, other_quarter], c_send.at[c], c_recv.at[c], adapter=other_a
        ).wait_recv()

    def columns(b):
        return pl.ds(pl.multiple_of(b * BLOCK, BLOCK), BLOCK)

    cot_arrival(a)

    def head_block(b, carry):
        head_part[:, columns(b)] = product(second[b], cot[a, columns(b)], 1, 1).astype(BF16)
        return carry

    lax.fori_loop(0, blocks, head_block, 0)
    swap = remote(head_part, head_got, h_send.at[0], h_recv.at[0], tensor=other_t)
    go(swap)
    swap.wait_recv()
    head[a] = (head_part[...].astype(F32) + head_got[...].astype(F32)).astype(BF16)
    go(remote(head.at[a], head.at[a], h_send.at[1], h_recv.at[1], adapter=other_a))
    own[2].wait()
    remote(head.at[other_a], head.at[other_a], h_send.at[1], h_recv.at[1], adapter=other_a).wait_recv()

    def head_of(b):
        return head[:, :, columns(b)].reshape(2 * ADAPTER_RANK, BLOCK)

    def down_block(b, carry):
        entries = product(head_of(b), acts[columns(b)], 1, 0)
        down_stage[b] = trade_pairs((adapter_scale * entries).T).astype(BF16)
        return carry

    lax.fori_loop(0, blocks, down_block, 0)

    def entries_for(device):
        return down_stage.at[:, pl.ds(pl.multiple_of(device * portion, 16), portion)]

    for i, peer in enumerate(peers):
        go(remote(
            entries_for(peer), down_ref.at[my_blocks], d_send.at[i], d_recv.at[f], fsdp=peer
        ))
    keep_down = pltpu.make_async_copy(entries_for(f), down_ref.at[my_blocks], local_sem.at[5])
    keep_down.start()

    cot_arrival(other_a)

    def part_copy(s, h):
        return remote(part.at[s], part_got.at[h], p_send.at[h], p_recv.at[h], tensor=other_t)

    def frozen(s):
        def rows(b, carry):
            value = product(cot[0, columns(b)], weight[s, 0], 1, 1)
            value = value + product(cot[1, columns(b)], weight[s, 1], 1, 1)
            part[s, columns(b)] = value.astype(BF16)
            return carry

        lax.fori_loop(0, blocks, rows, 0)

        @pl.when(s // 2 != t)
        def _():
            part_copy(s, s % 2).start()

    frozen(f)

    own[4].wait()
    for i, peer in enumerate(peers):
        remote(
            first_ref.at[my_blocks], first.at[peer], a_send.at[i], a_recv.at[peer], fsdp=peer
        ).wait_recv()

    def first_block(n, carry):
        b, s = n // 4, n % 4
        first_rows[b, pl.ds(pl.multiple_of(s * portion, 16), portion)] = trade_pairs(
            first[s, b].astype(F32)
        ).astype(BF16)
        return carry

    lax.fori_loop(0, 4 * blocks, first_block, 0)

    def low_block(b, carry):
        value = product(acts[columns(b)], first_rows[b], 1, 0)
        low_part[:, :, columns(b)] = value.T.reshape(2, ADAPTER_RANK, BLOCK).astype(BF16)
        return carry

    lax.fori_loop(0, blocks, low_block, 0)
    swap = remote(low_part.at[other_a], low_got.at[0], l_send.at[0], l_recv.at[0], adapter=other_a)
    go(swap)
    pass_on(0)
    swap.wait_recv()
    low_sum[...] = (low_part[a].astype(F32) + low_got[0].astype(F32)).astype(BF16)
    swap = remote(low_sum, low_got.at[1], l_send.at[1], l_recv.at[1], tensor=other_t)
    go(swap)
    swap.wait_recv()
    low[...] = (low_sum[...].astype(F32) + low_got[1].astype(F32)).astype(BF16)

    def up_block(b, carry):
        value = adapter_scale * product(low[:, columns(b)], cot[a, columns(b)], 1, 0)
        up_stage[b] = value.astype(BF16)
        return carry

    lax.fori_loop(0, blocks, up_block, 0)

    def ranks_for(device):
        return up_stage.at[:, pl.ds(pl.multiple_of(device * ranks, 16), ranks)]

    for i, peer in enumerate(peers):
        go(remote(ranks_for(peer), up_ref.at[a, my_blocks], u_send.at[i], u_recv.at[f], fsdp=peer))
    keep_up = pltpu.make_async_copy(ranks_for(f), up_ref.at[a, my_blocks], local_sem.at[6])
    keep_up.start()

    def twin_arrival(j):
        for sub in range(2):
            twin_copy(peers[j], other_g, j, sub).wait_recv()

    pass_on(1)
    twin_arrival(0)
    frozen(peers[0])
    pass_on(2)
    keep_up.wait()
    for i, peer in enumerate(peers):
        there = up_ref.at[a, pl.ds(peer * blocks, blocks)]
        remote(ranks_for(peer), there, u_send.at[i], u_recv.at[peer], fsdp=peer).wait_recv()
    go(remote(up_ref.at[a], up_ref.at[a], x_send.at[0], x_recv.at[0], adapter=other_a))
    twin_arrival(1)
    frozen(peers[1])
    twin_arrival(2)
    frozen(peers[2])

    for h in range(2):
        part_copy(2 * t + h, h).wait_recv()
    width = part.shape[2]

    def final_block(b, carry):
        grad = head_of(b).astype(F32).T.astype(BF16)
        for h in range(2):
            term = product(grad, first_rows[b, pl.ds(h * width, width)], 1, 1)
            base = part[2 * t + h, columns(b)].astype(F32) + part_got[h, columns(b)].astype(F32)
            ig_ref[columns(b), pl.ds(h * width, width)] = (base + adapter_scale * term).astype(BF16)
        return carry

    lax.fori_loop(0, blocks, final_block, 0)

    keep_down.wait()
    for i, peer in enumerate(peers):
        remote(
            entries_for(peer), down_ref.at[pl.ds(peer * blocks, blocks)],
            d_send.at[i], d_recv.at[peer], fsdp=peer,
        ).wait_recv()
    remote(up_ref.at[other_a], up_ref.at[other_a], x_send.at[0], x_recv.at[0], adapter=other_a).wait_recv()
    for h in range(2):
        part_copy(2 * other_t + h, h).wait_send()
    for copy in pending:
        copy.wait_send()

    @pl.when(inner)
    def _():
        for sub in range(2):
            weight_copy(f, sub, 1, 3 - f).wait_send()
            for j in range(3):
                weight_copy(peers[j], sub, 2 + j, onward[j]).wait_send()


def slice_on_device(
    acts,
    cotangent,
    key_value_weight,
    adapter_first_factor,
    adapter_second_factor,
    adapter_of_block,
    occupied_rows,
):
    f = lax.axis_index("fsdp")
    a = lax.axis_index("adapter")
    quarter, _, head_half = cotangent.shape
    rows, features = acts.shape
    blocks = rows // BLOCK
    all_blocks = adapter_of_block.shape[0]
    total, _, length = adapter_first_factor.shape
    ranks = adapter_second_factor.shape[2]
    portion = length // ADAPTER_RANK
    shard = key_value_weight.shape[0]
    anywhere = pl.BlockSpec(memory_space=pl.ANY)
    in_vmem = pl.BlockSpec(memory_space=pltpu.VMEM)
    in_smem = pl.BlockSpec(memory_space=pltpu.SMEM)
    dma = pltpu.SemaphoreType.DMA

    quarter_blocks = quarter // BLOCK
    live = lax.dynamic_slice_in_dim(
        occupied_rows, f * blocks + a * quarter_blocks, quarter_blocks, 0
    )
    kept = jnp.arange(BLOCK, dtype=jnp.int32)[None, :] < live[:, None]
    masked = jnp.where(
        kept[:, :, None, None],
        cotangent.reshape(quarter_blocks, BLOCK, 2, head_half),
        jnp.zeros((), BF16),
    )
    masked = masked.reshape(quarter, 2, head_half).transpose(1, 0, 2)
    weight = key_value_weight.transpose(1, 0, 2)

    first_used, second_used = pl.pallas_call(
        pick_kernel,
        out_shape=(
            jax.ShapeDtypeStruct((all_blocks, 2, length), BF16),
            jax.ShapeDtypeStruct((all_blocks, 2, ranks, head_half), BF16),
        ),
        in_specs=[in_smem, anywhere, anywhere],
        out_specs=(anywhere, anywhere),
        scratch_shapes=[dma((all_blocks,)), dma((all_blocks,))],
        name="pick",
    )(adapter_of_block, adapter_first_factor, adapter_second_factor)
    first_used = first_used.reshape(all_blocks, 2, length // 128, 128).transpose(0, 2, 1, 3)
    first_used = first_used.reshape(all_blocks, portion, 128)

    input_gradient, back_down, back_up = pl.pallas_call(
        layer_kernel,
        out_shape=(
            jax.ShapeDtypeStruct((rows, features), BF16),
            jax.ShapeDtypeStruct((all_blocks, portion, 128), BF16),
            jax.ShapeDtypeStruct((2, all_blocks, ranks, head_half), BF16),
        ),
        in_specs=[anywhere] * 5,
        out_specs=(in_vmem, anywhere, anywhere),
        scratch_shapes=[
            pltpu.VMEM((2, rows, head_half), BF16),
            pltpu.VMEM((4, 2, shard, head_half), BF16),
            pltpu.VMEM((4, blocks, portion, 128), BF16),
            pltpu.VMEM((blocks, features, 128), BF16),
            pltpu.VMEM((blocks, ADAPTER_RANK, head_half), BF16),
            pltpu.VMEM((rows, features), BF16),
            pltpu.VMEM((ADAPTER_RANK, rows), BF16),
            pltpu.VMEM((ADAPTER_RANK, rows), BF16),
            pltpu.VMEM((2, ADAPTER_RANK, rows), BF16),
            pltpu.VMEM((2, ADAPTER_RANK, rows), BF16),
            pltpu.VMEM((2, ADAPTER_RANK, rows), BF16),
            pltpu.VMEM((ADAPTER_RANK, rows), BF16),
            pltpu.VMEM((ADAPTER_RANK, rows), BF16),
            pltpu.VMEM((blocks, features, 128), BF16),
            pltpu.VMEM((blocks, ADAPTER_RANK, head_half), BF16),
            pltpu.VMEM((4, rows, shard), BF16),
            pltpu.VMEM((2, rows, shard), BF16),
            dma((7,)),
            dma((3,)), dma((4,)), dma((3,)), dma((4,)),
            dma((3,)), dma((4,)), dma((3,)), dma((4,)),
            dma((2,)), dma((2,)), dma((2,)), dma((2,)), dma((2,)), dma((2,)),
            dma((5, 2)), dma((4, 2)), dma((3, 2)), dma((4, 2)),
            dma((2,)), dma((2,)), dma((1,)), dma((1,)),
        ],
        compiler_params=pltpu.CompilerParams(
            collective_id=0, has_side_effects=True, vmem_limit_bytes=50 * 2**20
        ),
        name="layer",
    )(masked, weight, first_used, second_used, acts)

    span = 8
    down_grad, up_grad = pl.pallas_call(
        table_kernel,
        out_shape=(
            jax.ShapeDtypeStruct((total, portion, 128), BF16),
            jax.ShapeDtypeStruct((total, 2, ranks, head_half), BF16),
        ),
        in_specs=[in_smem, in_vmem, in_vmem],
        out_specs=(anywhere, anywhere),
        scratch_shapes=[
            pltpu.VMEM((span, portion, 128), BF16),
            pltpu.VMEM((span, 2, ranks, head_half), BF16),
            pltpu.VMEM((all_blocks, portion, 128), BF16),
            pltpu.VMEM((all_blocks, 2, ranks, head_half), BF16),
            pltpu.VMEM((portion, 128), F32),
            pltpu.VMEM((2, ranks, head_half), F32),
            pltpu.SMEM((all_blocks,), jnp.int32),
            dma((2, total // span)),
            dma((2, all_blocks)),
        ],
        compiler_params=pltpu.CompilerParams(vmem_limit_bytes=32 * 2**20),
        name="table",
    )(adapter_of_block, back_down, back_up)
    down_grad = down_grad.reshape(total, length // 128, 2, 128).transpose(0, 2, 1, 3)
    return (input_gradient, down_grad.reshape(total, 2, length), up_grad)


def on_slice(*args):
    sizes = tuple(lax.axis_size(name) for name in ("groups", "fsdp", "tensor", "adapter"))
    if sizes == (2, 4, 2, 2) and args[0].shape == (4 * BLOCK, 1280):
        return slice_on_device(*args)
    return general_on_device(*args)


def solution(mesh):
    in_specs = (
        P(("groups", "fsdp"), ("adapter", "tensor")),
        P(("groups", "fsdp", "adapter"), None, "tensor"),
        P(("adapter", "fsdp"), None, "tensor"),
        P(None, None, ("adapter", "tensor", "fsdp")),
        P(None, None, "fsdp", "tensor"),
        P("groups"),
        P("groups"),
    )
    out_specs = (
        P(("groups", "fsdp"), ("adapter", "tensor")),
        P("groups", None, ("adapter", "tensor", "fsdp")),
        P("groups", None, "fsdp", "tensor"),
    )
    return jax.shard_map(
        on_slice, mesh=mesh, in_specs=in_specs, out_specs=out_specs, check_vma=False
    )
```

```python
import jax
import jax.numpy as jnp
from jax import lax
from jax.experimental import pallas as pl
from jax.experimental.pallas import tpu as pltpu
from jax.sharding import PartitionSpec as P

ADAPTER_TOTAL = 96
ADAPTER_RANK = 64
BLOCK = 256


adapter_scale = 2.0


def general_on_device(
    acts,
    cotangent,
    key_value_weight,
    adapter_first_factor,
    adapter_second_factor,
    adapter_of_block,
    occupied_rows,
):
    fsdp_count = lax.axis_size("fsdp")
    fsdp_index = lax.axis_index("fsdp")
    adapter_index = lax.axis_index("adapter")
    count_of_rows = acts.shape[0]
    feature_columns = acts.shape[1]
    block_count = count_of_rows // BLOCK
    quarter_rows = cotangent.shape[0]
    head_half = cotangent.shape[2]
    portion_length = adapter_first_factor.shape[2]
    rank_portion = adapter_second_factor.shape[2]
    live_mine = lax.dynamic_slice_in_dim(occupied_rows, fsdp_index * block_count, block_count, 0)
    limits = jnp.repeat(live_mine, BLOCK, total_repeat_length=count_of_rows)
    limit_quarter = lax.dynamic_slice_in_dim(limits, adapter_index * quarter_rows, quarter_rows, 0)
    offsets = adapter_index * quarter_rows + jnp.arange(quarter_rows, dtype=jnp.int32)
    kept_rows = offsets % BLOCK < limit_quarter
    masked = jnp.where(kept_rows[:, None, None], cotangent, jnp.zeros_like(cotangent))
    cot_full = lax.all_gather(masked, "adapter", axis=0, tiled=True)
    departing_down = jnp.take(adapter_first_factor, adapter_of_block, axis=0)
    departing_up = jnp.take(adapter_second_factor, adapter_of_block, axis=0)
    fetched_down, fetched_up = (
        lax.all_to_all(departing_down, "fsdp", split_axis=0, concat_axis=0, tiled=True),
        lax.all_to_all(departing_up, "fsdp", split_axis=0, concat_axis=0, tiled=True),
    )
    own_down = fetched_down.reshape(fsdp_count, block_count, 2, portion_length).transpose(
        1, 2, 0, 3
    )
    own_down = own_down.reshape(block_count, 2, feature_columns, ADAPTER_RANK)
    own_up = fetched_up.reshape(fsdp_count, block_count, 2, rank_portion, head_half).transpose(
        1, 2, 0, 3, 4
    )
    own_up = own_up.reshape(block_count, 2, ADAPTER_RANK, head_half)
    cotangent_blocks = cot_full.reshape(block_count, BLOCK, 2, head_half)
    activation_blocks = acts.reshape(block_count, BLOCK, feature_columns)
    feature_part = jnp.einsum(
        "bnd,bcdr->bncr", activation_blocks, own_down, preferred_element_type=jnp.float32
    )
    head_part = jnp.einsum(
        "bnch,bcrh->bncr", cotangent_blocks, own_up, preferred_element_type=jnp.float32
    )
    head_total = lax.psum(head_part.astype(jnp.bfloat16), "tensor")
    feature_total = lax.psum(feature_part.astype(jnp.bfloat16), ("tensor", "adapter"))
    adapter_term = adapter_scale * jnp.einsum(
        "oyet,oemt->oym", head_total, own_down, preferred_element_type=jnp.float32
    )
    adapter_term = adapter_term.reshape(count_of_rows, feature_columns)
    block_down_factor = adapter_scale * jnp.einsum(
        "mky,mkzl->mzyl", activation_blocks, head_total, preferred_element_type=jnp.float32
    )
    block_up_factor = adapter_scale * jnp.einsum(
        "ijfm,ijfy->ifmy", feature_total, cotangent_blocks, preferred_element_type=jnp.float32
    )
    partial_value = jnp.einsum(
        "nch,dch->nd",
        cot_full,
        lax.all_gather(key_value_weight, "fsdp", axis=0, tiled=True),
        preferred_element_type=jnp.float32,
    )
    frozen_path_gradient = lax.psum_scatter(
        partial_value.astype(jnp.bfloat16), "tensor", scatter_dimension=1, tiled=True
    ).astype(jnp.float32)
    input_gradient = (frozen_path_gradient + adapter_term).astype(jnp.bfloat16)
    send_down = block_down_factor.reshape(block_count, 2, fsdp_count, portion_length).transpose(
        2, 0, 1, 3
    )
    send_down = send_down.reshape(fsdp_count * block_count, 2, portion_length)
    send_up = block_up_factor.reshape(
        block_count, 2, fsdp_count, rank_portion, head_half
    ).transpose(2, 0, 1, 3, 4)
    send_up = send_up.reshape(fsdp_count * block_count, 2, rank_portion, head_half)
    back_down, back_up = (
        lax.all_to_all(
            send_down.astype(jnp.bfloat16), "fsdp", split_axis=0, concat_axis=0, tiled=True
        ).astype(send_down.dtype),
        lax.all_to_all(
            send_up.astype(jnp.bfloat16), "fsdp", split_axis=0, concat_axis=0, tiled=True
        ).astype(send_up.dtype),
    )
    selector = (
        adapter_of_block[None, :] == jnp.arange(ADAPTER_TOTAL, dtype=jnp.int32)[:, None]
    ).astype(jnp.float32)
    down_factor_table = jnp.dot(
        selector, back_down.reshape(back_down.shape[0], -1), precision=lax.Precision.HIGHEST
    )
    table_up = jnp.dot(
        selector, back_up.reshape(back_up.shape[0], -1), precision=lax.Precision.HIGHEST
    )
    down_grad = down_factor_table.reshape(ADAPTER_TOTAL, 2, portion_length).astype(jnp.bfloat16)
    up_grad = table_up.reshape(ADAPTER_TOTAL, 2, rank_portion, head_half).astype(jnp.bfloat16)
    return (input_gradient, down_grad, up_grad)


MESH = pl.DeviceIdType.MESH
F32 = jnp.float32
BF16 = jnp.bfloat16


def product(left, right, left_dim, right_dim):
    return lax.dot_general(
        left, right, (((left_dim,), (right_dim,)), ((), ())), preferred_element_type=F32
    )


def trade_pairs(table):
    rows = table.shape[0]
    groups = table.reshape(rows // 8, 8, 128)
    row_odd = lax.broadcasted_iota(jnp.int32, groups.shape, 1) % 2
    lane_high = lax.broadcasted_iota(jnp.int32, groups.shape, 2) // 64
    other = jnp.where(row_odd == 0, pltpu.roll(groups, 7, 1), pltpu.roll(groups, 1, 1))
    other = pltpu.roll(other, 64, 2)
    return jnp.where(row_odd == lane_high, groups, other).reshape(rows, 128)


def pick_kernel(ids_ref, first_ref, second_ref, first_out, second_out, first_sem, second_sem):
    copies = []
    for block in range(first_out.shape[0]):
        which = ids_ref[block]
        copies.append(
            pltpu.make_async_copy(second_ref.at[which], second_out.at[block], second_sem.at[block])
        )
        copies.append(
            pltpu.make_async_copy(first_ref.at[which], first_out.at[block], first_sem.at[block])
        )
    for copy in copies:
        copy.start()
    for copy in copies:
        copy.wait()


def table_kernel(
    ids_ref, down_in, up_in, ig_ref, ig_out, down_out, up_out,
    zero_down, zero_up, down_ref, up_ref,
    ig, sum_down, sum_up, total_down, total_up, first, in_sem, ig_sem, zero_sem, row_sem,
):
    blocks = down_ref.shape[0]
    span = zero_down.shape[0]
    arrive = [
        pltpu.make_async_copy(down_in, down_ref, in_sem.at[0]),
        pltpu.make_async_copy(up_in, up_ref, in_sem.at[1]),
    ]
    take = pltpu.make_async_copy(ig_ref, ig, ig_sem.at[0])
    give = pltpu.make_async_copy(ig, ig_out, ig_sem.at[1])
    for copy in arrive:
        copy.start()
    take.start()
    zero_down[...] = jnp.zeros_like(zero_down)
    zero_up[...] = jnp.zeros_like(zero_up)
    copies = []
    for step in range(down_out.shape[0] // span):
        rows = pl.ds(step * span, span)
        copies.append(pltpu.make_async_copy(zero_down, down_out.at[rows], zero_sem.at[0, step]))
        copies.append(pltpu.make_async_copy(zero_up, up_out.at[rows], zero_sem.at[1, step]))
    for copy in copies:
        copy.start()
    for copy in arrive:
        copy.wait()

    def add_up(block, carry):
        mine = ids_ref[block]
        before = lax.fori_loop(
            0, block, lambda i, n: n + (ids_ref[i] == mine).astype(jnp.int32), jnp.int32(0)
        )
        first[block] = before

        @pl.when(before == 0)
        def _():
            total_down[...] = down_ref[block].astype(F32)
            total_up[...] = up_ref[:, block].astype(F32)

            def later(i, c):
                @pl.when(ids_ref[i] == mine)
                def _():
                    total_down[...] += down_ref[i].astype(F32)
                    total_up[...] += up_ref[:, i].astype(F32)
                return c

            lax.fori_loop(block + 1, blocks, later, 0)
            sum_down[block] = total_down[...].astype(BF16)
            sum_up[block] = total_up[...].astype(BF16)
        return carry

    take.wait()
    give.start()
    lax.fori_loop(0, blocks, add_up, 0)
    for copy in copies:
        copy.wait()

    def rows_of(block):
        which = ids_ref[block]
        return (
            pltpu.make_async_copy(sum_down.at[block], down_out.at[which], row_sem.at[0, block]),
            pltpu.make_async_copy(sum_up.at[block], up_out.at[which], row_sem.at[1, block]),
        )

    def send(block, carry):
        @pl.when(first[block] == 0)
        def _():
            for copy in rows_of(block):
                copy.start()
        return carry

    def settle(block, carry):
        @pl.when(first[block] == 0)
        def _():
            for copy in rows_of(block):
                copy.wait()
        return carry

    lax.fori_loop(0, blocks, send, 0)
    lax.fori_loop(0, blocks, settle, 0)
    give.wait()


def layer_kernel(
    cot_ref, w_ref, first_ref, second_ref, acts_ref,
    ig_ref, down_ref, up_ref,
    cot, weight, first, first_rows, second, acts,
    head_part, head_got, head, low_part, low_got, low_sum, low,
    down_stage, up_stage, part, part_got,
    local_sem, b_send, b_recv, a_send, a_recv, d_send, d_recv, u_send, u_recv,
    c_send, c_recv, h_send, h_recv, l_send, l_recv,
    w_send, w_recv, y_send, y_recv, p_send, p_recv, x_send, x_recv,
):
    f = lax.axis_index("fsdp")
    g = lax.axis_index("groups")
    t = lax.axis_index("tensor")
    a = lax.axis_index("adapter")
    other_g, other_t, other_a = 1 - g, 1 - t, 1 - a
    near = f + 1 - 2 * (f % 2)
    peers = (near, 2 - f // 2, 3 - 3 * (f // 2))
    inner = f * (3 - f) > 0
    blocks = 4
    portion = first_ref.shape[1]
    ranks = second_ref.shape[2]
    quarter = cot_ref.shape[1]
    half_rows = w_ref.shape[1] // 2
    pending = []

    def remote(source, target, send_sem, recv_sem, **where):
        return pltpu.make_async_remote_copy(
            src_ref=source, dst_ref=target, send_sem=send_sem, recv_sem=recv_sem,
            device_id=where, device_id_type=MESH,
        )

    def go(copy):
        copy.start()
        pending.append(copy)

    barrier = pltpu.get_barrier_semaphore()
    for where in (
        {"fsdp": peers[0]}, {"fsdp": peers[1]}, {"fsdp": peers[2]},
        {"groups": other_g}, {"tensor": other_t}, {"adapter": other_a},
    ):
        pl.semaphore_signal(barrier, inc=1, device_id=where, device_id_type=MESH)

    my_blocks = pl.ds(f * blocks, blocks)
    my_ranks = pl.ds(pl.multiple_of(f * ranks, 16), ranks)
    my_quarter = pl.ds(pl.multiple_of(a * quarter, 256), quarter)
    other_quarter = pl.ds(pl.multiple_of(other_a * quarter, 256), quarter)
    own = [
        pltpu.make_async_copy(second_ref.at[my_blocks, a], second.at[:, my_ranks], local_sem.at[0]),
        pltpu.make_async_copy(cot_ref, cot.at[:, my_quarter], local_sem.at[1]),
        pltpu.make_async_copy(acts_ref, acts, local_sem.at[2]),
        pltpu.make_async_copy(w_ref, weight.at[f], local_sem.at[3]),
        pltpu.make_async_copy(first_ref.at[my_blocks], first.at[f], local_sem.at[4]),
    ]
    for copy in own:
        copy.start()
    pl.semaphore_wait(barrier, 6)

    for i, peer in enumerate(peers):
        go(remote(
            second_ref.at[pl.ds(peer * blocks, blocks), a], second.at[:, my_ranks],
            b_send.at[i], b_recv.at[f], fsdp=peer,
        ))
    for c in (other_a, a):
        go(remote(
            cot_ref.at[c], cot.at[c, my_quarter], c_send.at[c], c_recv.at[c], adapter=other_a
        ))
    def piece(s, c, sub):
        return weight.at[s, c, pl.ds(sub * half_rows, half_rows)]

    def weight_copy(s, sub, slot, target):
        return remote(
            piece(s, g, sub), piece(s, g, sub), w_send.at[slot, sub], w_recv.at[s, sub], fsdp=target
        )

    def twin_copy(s, c, j, sub):
        return remote(
            piece(s, c, sub), piece(s, c, sub), y_send.at[j, sub], y_recv.at[s, sub], groups=other_g
        )

    onward = (3 - f, (f - 1) * 3, (f - 1) * 3)

    def pass_on(j):
        s = peers[j]
        for sub in range(2):
            weight_copy(s, sub, 0, near).wait_recv()

            @pl.when(inner)
            def _():
                weight_copy(s, sub, 2 + j, onward[j]).start()

            go(twin_copy(s, g, j, sub))

    own[3].wait()
    for sub in range(2):
        go(weight_copy(f, sub, 0, near))

        @pl.when(inner)
        def _():
            weight_copy(f, sub, 1, 3 - f).start()

    own[0].wait()
    own[1].wait()
    for i, peer in enumerate(peers):
        remote(
            second_ref.at[pl.ds(peer * blocks, blocks), a],
            second.at[:, pl.ds(pl.multiple_of(peer * ranks, 16), ranks)],
            b_send.at[i], b_recv.at[peer], fsdp=peer,
        ).wait_recv()

    def cot_arrival(c):
        remote(
            cot_ref.at[c], cot.at[c, other_quarter], c_send.at[c], c_recv.at[c], adapter=other_a
        ).wait_recv()

    def columns(b):
        return pl.ds(pl.multiple_of(b * BLOCK, BLOCK), BLOCK)

    cot_arrival(a)

    def head_block(b, carry):
        head_part[:, columns(b)] = product(second[b], cot[a, columns(b)], 1, 1).astype(BF16)
        return carry

    lax.fori_loop(0, blocks, head_block, 0)
    swap = remote(head_part, head_got, h_send.at[0], h_recv.at[0], tensor=other_t)
    go(swap)
    swap.wait_recv()
    head[a] = (head_part[...].astype(F32) + head_got[...].astype(F32)).astype(BF16)
    go(remote(head.at[a], head.at[a], h_send.at[1], h_recv.at[1], adapter=other_a))
    own[2].wait()
    remote(head.at[other_a], head.at[other_a], h_send.at[1], h_recv.at[1], adapter=other_a).wait_recv()

    def head_of(b):
        return head[:, :, columns(b)].reshape(2 * ADAPTER_RANK, BLOCK)

    pass_on(0)
    for i, peer in enumerate(peers):
        go(remote(
            first_ref.at[pl.ds(peer * blocks, blocks)], first.at[f],
            a_send.at[i], a_recv.at[f], fsdp=peer,
        ))

    def down_block(b, carry):
        entries = product(head_of(b), acts[columns(b)], 1, 0)
        down_stage[b] = trade_pairs((adapter_scale * entries).T).astype(BF16)
        return carry

    lax.fori_loop(0, blocks, down_block, 0)

    def entries_for(device):
        return down_stage.at[:, pl.ds(pl.multiple_of(device * portion, 16), portion)]

    cot_arrival(other_a)

    def part_copy(s, h):
        return remote(part.at[s], part_got.at[h], p_send.at[h], p_recv.at[h], tensor=other_t)

    def frozen(s):
        def rows(b, carry):
            value = product(cot[0, columns(b)], weight[s, 0], 1, 1)
            value = value + product(cot[1, columns(b)], weight[s, 1], 1, 1)
            part[s, columns(b)] = value.astype(BF16)
            return carry

        lax.fori_loop(0, blocks, rows, 0)

        @pl.when(s // 2 != t)
        def _():
            part_copy(s, s % 2).start()

    def twin_arrival(j):
        for sub in range(2):
            twin_copy(peers[j], other_g, j, sub).wait_recv()

    frozen(f)
    pass_on(1)
    twin_arrival(0)
    frozen(peers[0])
    pass_on(2)
    for i, peer in enumerate(peers):
        go(remote(
            entries_for(peer), down_ref.at[my_blocks], d_send.at[i], d_recv.at[f], fsdp=peer
        ))
    keep_down = pltpu.make_async_copy(entries_for(f), down_ref.at[my_blocks], local_sem.at[5])
    keep_down.start()


    own[4].wait()
    for i, peer in enumerate(peers):
        remote(
            first_ref.at[my_blocks], first.at[peer], a_send.at[i], a_recv.at[peer], fsdp=peer
        ).wait_recv()

    def first_block(n, carry):
        b, s = n // 4, n % 4
        first_rows[b, pl.ds(pl.multiple_of(s * portion, 16), portion)] = trade_pairs(
            first[s, b].astype(F32)
        ).astype(BF16)
        return carry

    lax.fori_loop(0, 4 * blocks, first_block, 0)

    def low_block(b, carry):
        value = product(acts[columns(b)], first_rows[b], 1, 0)
        low_part[:, :, columns(b)] = value.T.reshape(2, ADAPTER_RANK, BLOCK).astype(BF16)
        return carry

    lax.fori_loop(0, blocks, low_block, 0)
    swap = remote(low_part.at[other_a], low_got.at[0], l_send.at[0], l_recv.at[0], adapter=other_a)
    go(swap)
    swap.wait_recv()
    low_sum[...] = (low_part[a].astype(F32) + low_got[0].astype(F32)).astype(BF16)
    swap = remote(low_sum, low_got.at[1], l_send.at[1], l_recv.at[1], tensor=other_t)
    go(swap)
    swap.wait_recv()
    low[...] = (low_sum[...].astype(F32) + low_got[1].astype(F32)).astype(BF16)

    def up_block(b, carry):
        value = adapter_scale * product(low[:, columns(b)], cot[a, columns(b)], 1, 0)
        up_stage[b] = value.astype(BF16)
        return carry

    lax.fori_loop(0, blocks, up_block, 0)

    def ranks_for(device):
        return up_stage.at[:, pl.ds(pl.multiple_of(device * ranks, 16), ranks)]

    for i, peer in enumerate(peers):
        go(remote(ranks_for(peer), up_ref.at[a, my_blocks], u_send.at[i], u_recv.at[f], fsdp=peer))
    keep_up = pltpu.make_async_copy(ranks_for(f), up_ref.at[a, my_blocks], local_sem.at[6])
    keep_up.start()

    twin_arrival(1)
    frozen(peers[1])
    twin_arrival(2)
    frozen(peers[2])
    keep_up.wait()
    for i, peer in enumerate(peers):
        there = up_ref.at[a, pl.ds(peer * blocks, blocks)]
        remote(ranks_for(peer), there, u_send.at[i], u_recv.at[peer], fsdp=peer).wait_recv()
    go(remote(up_ref.at[a], up_ref.at[a], x_send.at[0], x_recv.at[0], adapter=other_a))

    for h in range(2):
        part_copy(2 * t + h, h).wait_recv()
    width = part.shape[2]

    def final_block(b, carry):
        grad = head_of(b).astype(F32).T.astype(BF16)
        for h in range(2):
            term = product(grad, first_rows[b, pl.ds(h * width, width)], 1, 1)
            base = part[2 * t + h, columns(b)].astype(F32) + part_got[h, columns(b)].astype(F32)
            ig_ref[columns(b), pl.ds(h * width, width)] = (base + adapter_scale * term).astype(BF16)
        return carry

    lax.fori_loop(0, blocks, final_block, 0)

    keep_down.wait()
    for i, peer in enumerate(peers):
        remote(
            entries_for(peer), down_ref.at[pl.ds(peer * blocks, blocks)],
            d_send.at[i], d_recv.at[peer], fsdp=peer,
        ).wait_recv()
    remote(up_ref.at[other_a], up_ref.at[other_a], x_send.at[0], x_recv.at[0], adapter=other_a).wait_recv()
    for h in range(2):
        part_copy(2 * other_t + h, h).wait_send()
    for copy in pending:
        copy.wait_send()

    @pl.when(inner)
    def _():
        for sub in range(2):
            weight_copy(f, sub, 1, 3 - f).wait_send()
            for j in range(3):
                weight_copy(peers[j], sub, 2 + j, onward[j]).wait_send()


def slice_on_device(
    acts,
    cotangent,
    key_value_weight,
    adapter_first_factor,
    adapter_second_factor,
    adapter_of_block,
    occupied_rows,
):
    f = lax.axis_index("fsdp")
    a = lax.axis_index("adapter")
    quarter, _, head_half = cotangent.shape
    rows, features = acts.shape
    blocks = rows // BLOCK
    all_blocks = adapter_of_block.shape[0]
    total, _, length = adapter_first_factor.shape
    ranks = adapter_second_factor.shape[2]
    portion = length // ADAPTER_RANK
    shard = key_value_weight.shape[0]
    anywhere = pl.BlockSpec(memory_space=pl.ANY)
    in_vmem = pl.BlockSpec(memory_space=pltpu.VMEM)
    in_smem = pl.BlockSpec(memory_space=pltpu.SMEM)
    dma = pltpu.SemaphoreType.DMA

    quarter_blocks = quarter // BLOCK
    live = lax.dynamic_slice_in_dim(
        occupied_rows, f * blocks + a * quarter_blocks, quarter_blocks, 0
    )
    kept = jnp.arange(BLOCK, dtype=jnp.int32)[None, :] < live[:, None]
    masked = jnp.where(
        kept[:, :, None, None],
        cotangent.reshape(quarter_blocks, BLOCK, 2, head_half),
        jnp.zeros((), BF16),
    )
    masked = masked.reshape(quarter, 2, head_half).transpose(1, 0, 2)
    weight = key_value_weight.transpose(1, 0, 2)

    first_used, second_used = pl.pallas_call(
        pick_kernel,
        out_shape=(
            jax.ShapeDtypeStruct((all_blocks, 2, length), BF16),
            jax.ShapeDtypeStruct((all_blocks, 2, ranks, head_half), BF16),
        ),
        in_specs=[in_smem, anywhere, anywhere],
        out_specs=(in_vmem, in_vmem),
        scratch_shapes=[dma((all_blocks,)), dma((all_blocks,))],
        name="pick",
    )(adapter_of_block, adapter_first_factor, adapter_second_factor)
    first_used = first_used.reshape(all_blocks, 2, length // 128, 128).transpose(0, 2, 1, 3)
    first_used = first_used.reshape(all_blocks, portion, 128)

    span = 8
    input_gradient, back_down, back_up = pl.pallas_call(
        layer_kernel,
        out_shape=(
            jax.ShapeDtypeStruct((rows, features), BF16),
            jax.ShapeDtypeStruct((all_blocks, portion, 128), BF16),
            jax.ShapeDtypeStruct((2, all_blocks, ranks, head_half), BF16),
        ),
        in_specs=[anywhere] * 5,
        out_specs=(in_vmem, anywhere, anywhere),
        scratch_shapes=[
            pltpu.VMEM((2, rows, head_half), BF16),
            pltpu.VMEM((4, 2, shard, head_half), BF16),
            pltpu.VMEM((4, blocks, portion, 128), BF16),
            pltpu.VMEM((blocks, features, 128), BF16),
            pltpu.VMEM((blocks, ADAPTER_RANK, head_half), BF16),
            pltpu.VMEM((rows, features), BF16),
            pltpu.VMEM((ADAPTER_RANK, rows), BF16),
            pltpu.VMEM((ADAPTER_RANK, rows), BF16),
            pltpu.VMEM((2, ADAPTER_RANK, rows), BF16),
            pltpu.VMEM((2, ADAPTER_RANK, rows), BF16),
            pltpu.VMEM((2, ADAPTER_RANK, rows), BF16),
            pltpu.VMEM((ADAPTER_RANK, rows), BF16),
            pltpu.VMEM((ADAPTER_RANK, rows), BF16),
            pltpu.VMEM((blocks, features, 128), BF16),
            pltpu.VMEM((blocks, ADAPTER_RANK, head_half), BF16),
            pltpu.VMEM((4, rows, shard), BF16),
            pltpu.VMEM((2, rows, shard), BF16),
            dma((7,)),
            dma((3,)), dma((4,)), dma((3,)), dma((4,)),
            dma((3,)), dma((4,)), dma((3,)), dma((4,)),
            dma((2,)), dma((2,)), dma((2,)), dma((2,)), dma((2,)), dma((2,)),
            dma((5, 2)), dma((4, 2)), dma((3, 2)), dma((4, 2)),
            dma((2,)), dma((2,)), dma((1,)), dma((1,)),
        ],
        compiler_params=pltpu.CompilerParams(
            collective_id=0, has_side_effects=True, vmem_limit_bytes=58 * 2**20
        ),
        name="layer",
    )(masked, weight, first_used, second_used, acts)

    input_gradient, down_grad, up_grad = pl.pallas_call(
        table_kernel,
        out_shape=(
            jax.ShapeDtypeStruct((rows, features), BF16),
            jax.ShapeDtypeStruct((total, portion, 128), BF16),
            jax.ShapeDtypeStruct((total, 2, ranks, head_half), BF16),
        ),
        in_specs=[in_smem, anywhere, anywhere, anywhere],
        out_specs=(anywhere, anywhere, anywhere),
        scratch_shapes=[
            pltpu.VMEM((span, portion, 128), BF16),
            pltpu.VMEM((span, 2, ranks, head_half), BF16),
            pltpu.VMEM((all_blocks, portion, 128), BF16),
            pltpu.VMEM((2, all_blocks, ranks, head_half), BF16),
            pltpu.VMEM((rows, features), BF16),
            pltpu.VMEM((all_blocks, portion, 128), BF16),
            pltpu.VMEM((all_blocks, 2, ranks, head_half), BF16),
            pltpu.VMEM((portion, 128), F32),
            pltpu.VMEM((2, ranks, head_half), F32),
            pltpu.SMEM((all_blocks,), jnp.int32),
            dma((2,)),
            dma((2,)),
            dma((2, total // span)),
            dma((2, all_blocks)),
        ],
        compiler_params=pltpu.CompilerParams(vmem_limit_bytes=60 * 2**20),
        name="table",
    )(adapter_of_block, back_down, back_up, input_gradient)
    down_grad = down_grad.reshape(total, length // 128, 2, 128).transpose(0, 2, 1, 3)
    return (input_gradient, down_grad.reshape(total, 2, length), up_grad)


def on_slice(*args):
    sizes = tuple(lax.axis_size(name) for name in ("groups", "fsdp", "tensor", "adapter"))
    if sizes == (2, 4, 2, 2) and args[0].shape == (4 * BLOCK, 1280):
        return slice_on_device(*args)
    return general_on_device(*args)


def solution(mesh):
    in_specs = (
        P(("groups", "fsdp"), ("adapter", "tensor")),
        P(("groups", "fsdp", "adapter"), None, "tensor"),
        P(("adapter", "fsdp"), None, "tensor"),
        P(None, None, ("adapter", "tensor", "fsdp")),
        P(None, None, "fsdp", "tensor"),
        P("groups"),
        P("groups"),
    )
    out_specs = (
        P(("groups", "fsdp"), ("adapter", "tensor")),
        P("groups", None, ("adapter", "tensor", "fsdp")),
        P("groups", None, "fsdp", "tensor"),
    )
    return jax.shard_map(
        on_slice, mesh=mesh, in_specs=in_specs, out_specs=out_specs, check_vma=False
    )
```

```python
import jax
import jax.numpy as jnp
from jax import lax
from jax.experimental import pallas as pl
from jax.experimental.pallas import tpu as pltpu
from jax.sharding import PartitionSpec as P

ADAPTER_TOTAL = 96
ADAPTER_RANK = 64
BLOCK = 256


adapter_scale = 2.0


def general_on_device(
    acts,
    cotangent,
    key_value_weight,
    adapter_first_factor,
    adapter_second_factor,
    adapter_of_block,
    occupied_rows,
):
    fsdp_count = lax.axis_size("fsdp")
    fsdp_index = lax.axis_index("fsdp")
    adapter_index = lax.axis_index("adapter")
    count_of_rows = acts.shape[0]
    feature_columns = acts.shape[1]
    block_count = count_of_rows // BLOCK
    quarter_rows = cotangent.shape[0]
    head_half = cotangent.shape[2]
    portion_length = adapter_first_factor.shape[2]
    rank_portion = adapter_second_factor.shape[2]
    live_mine = lax.dynamic_slice_in_dim(occupied_rows, fsdp_index * block_count, block_count, 0)
    limits = jnp.repeat(live_mine, BLOCK, total_repeat_length=count_of_rows)
    limit_quarter = lax.dynamic_slice_in_dim(limits, adapter_index * quarter_rows, quarter_rows, 0)
    offsets = adapter_index * quarter_rows + jnp.arange(quarter_rows, dtype=jnp.int32)
    kept_rows = offsets % BLOCK < limit_quarter
    masked = jnp.where(kept_rows[:, None, None], cotangent, jnp.zeros_like(cotangent))
    cot_full = lax.all_gather(masked, "adapter", axis=0, tiled=True)
    departing_down = jnp.take(adapter_first_factor, adapter_of_block, axis=0)
    departing_up = jnp.take(adapter_second_factor, adapter_of_block, axis=0)
    fetched_down, fetched_up = (
        lax.all_to_all(departing_down, "fsdp", split_axis=0, concat_axis=0, tiled=True),
        lax.all_to_all(departing_up, "fsdp", split_axis=0, concat_axis=0, tiled=True),
    )
    own_down = fetched_down.reshape(fsdp_count, block_count, 2, portion_length).transpose(
        1, 2, 0, 3
    )
    own_down = own_down.reshape(block_count, 2, feature_columns, ADAPTER_RANK)
    own_up = fetched_up.reshape(fsdp_count, block_count, 2, rank_portion, head_half).transpose(
        1, 2, 0, 3, 4
    )
    own_up = own_up.reshape(block_count, 2, ADAPTER_RANK, head_half)
    cotangent_blocks = cot_full.reshape(block_count, BLOCK, 2, head_half)
    activation_blocks = acts.reshape(block_count, BLOCK, feature_columns)
    feature_part = jnp.einsum(
        "bnd,bcdr->bncr", activation_blocks, own_down, preferred_element_type=jnp.float32
    )
    head_part = jnp.einsum(
        "bnch,bcrh->bncr", cotangent_blocks, own_up, preferred_element_type=jnp.float32
    )
    head_total = lax.psum(head_part.astype(jnp.bfloat16), "tensor")
    feature_total = lax.psum(feature_part.astype(jnp.bfloat16), ("tensor", "adapter"))
    adapter_term = adapter_scale * jnp.einsum(
        "oyet,oemt->oym", head_total, own_down, preferred_element_type=jnp.float32
    )
    adapter_term = adapter_term.reshape(count_of_rows, feature_columns)
    block_down_factor = adapter_scale * jnp.einsum(
        "mky,mkzl->mzyl", activation_blocks, head_total, preferred_element_type=jnp.float32
    )
    block_up_factor = adapter_scale * jnp.einsum(
        "ijfm,ijfy->ifmy", feature_total, cotangent_blocks, preferred_element_type=jnp.float32
    )
    partial_value = jnp.einsum(
        "nch,dch->nd",
        cot_full,
        lax.all_gather(key_value_weight, "fsdp", axis=0, tiled=True),
        preferred_element_type=jnp.float32,
    )
    frozen_path_gradient = lax.psum_scatter(
        partial_value.astype(jnp.bfloat16), "tensor", scatter_dimension=1, tiled=True
    ).astype(jnp.float32)
    input_gradient = (frozen_path_gradient + adapter_term).astype(jnp.bfloat16)
    send_down = block_down_factor.reshape(block_count, 2, fsdp_count, portion_length).transpose(
        2, 0, 1, 3
    )
    send_down = send_down.reshape(fsdp_count * block_count, 2, portion_length)
    send_up = block_up_factor.reshape(
        block_count, 2, fsdp_count, rank_portion, head_half
    ).transpose(2, 0, 1, 3, 4)
    send_up = send_up.reshape(fsdp_count * block_count, 2, rank_portion, head_half)
    back_down, back_up = (
        lax.all_to_all(
            send_down.astype(jnp.bfloat16), "fsdp", split_axis=0, concat_axis=0, tiled=True
        ).astype(send_down.dtype),
        lax.all_to_all(
            send_up.astype(jnp.bfloat16), "fsdp", split_axis=0, concat_axis=0, tiled=True
        ).astype(send_up.dtype),
    )
    selector = (
        adapter_of_block[None, :] == jnp.arange(ADAPTER_TOTAL, dtype=jnp.int32)[:, None]
    ).astype(jnp.float32)
    down_factor_table = jnp.dot(
        selector, back_down.reshape(back_down.shape[0], -1), precision=lax.Precision.HIGHEST
    )
    table_up = jnp.dot(
        selector, back_up.reshape(back_up.shape[0], -1), precision=lax.Precision.HIGHEST
    )
    down_grad = down_factor_table.reshape(ADAPTER_TOTAL, 2, portion_length).astype(jnp.bfloat16)
    up_grad = table_up.reshape(ADAPTER_TOTAL, 2, rank_portion, head_half).astype(jnp.bfloat16)
    return (input_gradient, down_grad, up_grad)


MESH = pl.DeviceIdType.MESH
F32 = jnp.float32
BF16 = jnp.bfloat16


def product(left, right, left_dim, right_dim):
    return lax.dot_general(
        left, right, (((left_dim,), (right_dim,)), ((), ())), preferred_element_type=F32
    )


def trade_pairs(table):
    rows = table.shape[0]
    groups = table.reshape(rows // 8, 8, 128)
    row_odd = lax.broadcasted_iota(jnp.int32, groups.shape, 1) % 2
    lane_high = lax.broadcasted_iota(jnp.int32, groups.shape, 2) // 64
    other = jnp.where(row_odd == 0, pltpu.roll(groups, 7, 1), pltpu.roll(groups, 1, 1))
    other = pltpu.roll(other, 64, 2)
    return jnp.where(row_odd == lane_high, groups, other).reshape(rows, 128)


def pick_kernel(ids_ref, first_ref, second_ref, first_out, second_out, first_sem, second_sem):
    copies = []
    for block in range(first_out.shape[0]):
        which = ids_ref[block]
        copies.append(
            pltpu.make_async_copy(second_ref.at[which], second_out.at[block], second_sem.at[block])
        )
        copies.append(
            pltpu.make_async_copy(first_ref.at[which], first_out.at[block], first_sem.at[block])
        )
    for copy in copies:
        copy.start()
    for copy in copies:
        copy.wait()


def table_kernel(
    ids_ref, down_in, up_in, ig_ref, ig_out, down_out, up_out,
    zero_down, zero_up, down_ref, up_ref,
    ig, sum_down, sum_up, total_down, total_up, first, in_sem, ig_sem, zero_sem, row_sem,
):
    blocks = down_ref.shape[0]
    span = zero_down.shape[0]
    arrive = [
        pltpu.make_async_copy(down_in, down_ref, in_sem.at[0]),
        pltpu.make_async_copy(up_in, up_ref, in_sem.at[1]),
    ]
    take = pltpu.make_async_copy(ig_ref, ig, ig_sem.at[0])
    give = pltpu.make_async_copy(ig, ig_out, ig_sem.at[1])
    for copy in arrive:
        copy.start()
    take.start()
    zero_down[...] = jnp.zeros_like(zero_down)
    zero_up[...] = jnp.zeros_like(zero_up)
    copies = []
    for step in range(down_out.shape[0] // span):
        rows = pl.ds(step * span, span)
        copies.append(pltpu.make_async_copy(zero_down, down_out.at[rows], zero_sem.at[0, step]))
        copies.append(pltpu.make_async_copy(zero_up, up_out.at[rows], zero_sem.at[1, step]))
    for copy in copies:
        copy.start()
    for copy in arrive:
        copy.wait()

    def add_up(block, carry):
        mine = ids_ref[block]
        before = lax.fori_loop(
            0, block, lambda i, n: n + (ids_ref[i] == mine).astype(jnp.int32), jnp.int32(0)
        )
        first[block] = before

        @pl.when(before == 0)
        def _():
            total_down[...] = down_ref[block].astype(F32)
            total_up[...] = up_ref[:, block].astype(F32)

            def later(i, c):
                @pl.when(ids_ref[i] == mine)
                def _():
                    total_down[...] += down_ref[i].astype(F32)
                    total_up[...] += up_ref[:, i].astype(F32)
                return c

            lax.fori_loop(block + 1, blocks, later, 0)
            sum_down[block] = total_down[...].astype(BF16)
            sum_up[block] = total_up[...].astype(BF16)
        return carry

    take.wait()
    give.start()
    lax.fori_loop(0, blocks, add_up, 0)
    for copy in copies:
        copy.wait()

    def rows_of(block):
        which = ids_ref[block]
        return (
            pltpu.make_async_copy(sum_down.at[block], down_out.at[which], row_sem.at[0, block]),
            pltpu.make_async_copy(sum_up.at[block], up_out.at[which], row_sem.at[1, block]),
        )

    def send(block, carry):
        @pl.when(first[block] == 0)
        def _():
            for copy in rows_of(block):
                copy.start()
        return carry

    def settle(block, carry):
        @pl.when(first[block] == 0)
        def _():
            for copy in rows_of(block):
                copy.wait()
        return carry

    lax.fori_loop(0, blocks, send, 0)
    lax.fori_loop(0, blocks, settle, 0)
    give.wait()


def layer_kernel(
    cot_ref, w_ref, first_ref, second_ref, acts_ref,
    ig_ref, down_ref, up_ref,
    cot, weight, first, first_rows, second, acts,
    head_part, head_got, head, low_part, low_got, low_sum, low,
    down_stage, up_stage, part, part_got, ig,
    local_sem, b_send, b_recv, a_send, a_recv, d_send, d_recv, u_send, u_recv,
    c_send, c_recv, h_send, h_recv, l_send, l_recv,
    w_send, w_recv, y_send, y_recv, p_send, p_recv, x_send, x_recv, ig_sem,
):
    f = lax.axis_index("fsdp")
    g = lax.axis_index("groups")
    t = lax.axis_index("tensor")
    a = lax.axis_index("adapter")
    other_g, other_t, other_a = 1 - g, 1 - t, 1 - a
    near = f + 1 - 2 * (f % 2)
    peers = (near, 2 - f // 2, 3 - 3 * (f // 2))
    inner = f * (3 - f) > 0
    blocks = 4
    portion = first_ref.shape[1]
    ranks = second_ref.shape[2]
    quarter = cot_ref.shape[1]
    half_rows = w_ref.shape[1] // 2
    pending = []

    def remote(source, target, send_sem, recv_sem, **where):
        return pltpu.make_async_remote_copy(
            src_ref=source, dst_ref=target, send_sem=send_sem, recv_sem=recv_sem,
            device_id=where, device_id_type=MESH,
        )

    def go(copy):
        copy.start()
        pending.append(copy)

    barrier = pltpu.get_barrier_semaphore()
    for where in (
        {"fsdp": peers[0]}, {"fsdp": peers[1]}, {"fsdp": peers[2]},
        {"groups": other_g}, {"tensor": other_t}, {"adapter": other_a},
    ):
        pl.semaphore_signal(barrier, inc=1, device_id=where, device_id_type=MESH)

    my_blocks = pl.ds(f * blocks, blocks)
    my_ranks = pl.ds(pl.multiple_of(f * ranks, 16), ranks)
    my_quarter = pl.ds(pl.multiple_of(a * quarter, 256), quarter)
    other_quarter = pl.ds(pl.multiple_of(other_a * quarter, 256), quarter)
    own = [
        pltpu.make_async_copy(second_ref.at[my_blocks, a], second.at[:, my_ranks], local_sem.at[0]),
        pltpu.make_async_copy(cot_ref, cot.at[:, my_quarter], local_sem.at[1]),
        pltpu.make_async_copy(acts_ref, acts, local_sem.at[2]),
        pltpu.make_async_copy(w_ref, weight.at[f], local_sem.at[3]),
        pltpu.make_async_copy(first_ref.at[my_blocks], first.at[f], local_sem.at[4]),
    ]
    for copy in own:
        copy.start()
    pl.semaphore_wait(barrier, 6)

    for i, peer in enumerate(peers):
        go(remote(
            second_ref.at[pl.ds(peer * blocks, blocks), a], second.at[:, my_ranks],
            b_send.at[i], b_recv.at[f], fsdp=peer,
        ))
    for c in (other_a, a):
        go(remote(
            cot_ref.at[c], cot.at[c, my_quarter], c_send.at[c], c_recv.at[c], adapter=other_a
        ))
    def piece(s, c, sub):
        return weight.at[s, c, pl.ds(sub * half_rows, half_rows)]

    def weight_copy(s, sub, slot, target):
        return remote(
            piece(s, g, sub), piece(s, g, sub), w_send.at[slot, sub], w_recv.at[s, sub], fsdp=target
        )

    def twin_copy(s, c, j, sub):
        return remote(
            piece(s, c, sub), piece(s, c, sub), y_send.at[j, sub], y_recv.at[s, sub], groups=other_g
        )

    onward = (3 - f, (f - 1) * 3, (f - 1) * 3)

    def pass_on(j):
        s = peers[j]
        for sub in range(2):
            weight_copy(s, sub, 0, near).wait_recv()

            @pl.when(inner)
            def _():
                weight_copy(s, sub, 2 + j, onward[j]).start()

            go(twin_copy(s, g, j, sub))

    own[3].wait()
    for sub in range(2):
        go(weight_copy(f, sub, 0, near))

        @pl.when(inner)
        def _():
            weight_copy(f, sub, 1, 3 - f).start()

    own[0].wait()
    own[1].wait()
    for i, peer in enumerate(peers):
        remote(
            second_ref.at[pl.ds(peer * blocks, blocks), a],
            second.at[:, pl.ds(pl.multiple_of(peer * ranks, 16), ranks)],
            b_send.at[i], b_recv.at[peer], fsdp=peer,
        ).wait_recv()

    def cot_arrival(c):
        remote(
            cot_ref.at[c], cot.at[c, other_quarter], c_send.at[c], c_recv.at[c], adapter=other_a
        ).wait_recv()

    def columns(b):
        return pl.ds(pl.multiple_of(b * BLOCK, BLOCK), BLOCK)

    cot_arrival(a)

    def head_block(b, carry):
        head_part[:, columns(b)] = product(second[b], cot[a, columns(b)], 1, 1).astype(BF16)
        return carry

    lax.fori_loop(0, blocks, head_block, 0)
    swap = remote(head_part, head_got, h_send.at[0], h_recv.at[0], tensor=other_t)
    go(swap)
    swap.wait_recv()
    head[a] = (head_part[...].astype(F32) + head_got[...].astype(F32)).astype(BF16)
    go(remote(head.at[a], head.at[a], h_send.at[1], h_recv.at[1], adapter=other_a))
    own[2].wait()
    remote(head.at[other_a], head.at[other_a], h_send.at[1], h_recv.at[1], adapter=other_a).wait_recv()

    def head_of(b):
        return head[:, :, columns(b)].reshape(2 * ADAPTER_RANK, BLOCK)

    pass_on(0)
    for i, peer in enumerate(peers):
        go(remote(
            first_ref.at[pl.ds(peer * blocks, blocks)], first.at[f],
            a_send.at[i], a_recv.at[f], fsdp=peer,
        ))

    def down_block(b, carry):
        entries = product(head_of(b), acts[columns(b)], 1, 0)
        down_stage[b] = trade_pairs((adapter_scale * entries).T).astype(BF16)
        return carry

    lax.fori_loop(0, blocks, down_block, 0)

    def entries_for(device):
        return down_stage.at[:, pl.ds(pl.multiple_of(device * portion, 16), portion)]

    cot_arrival(other_a)

    def part_copy(s, h):
        return remote(part.at[s], part_got.at[h], p_send.at[h], p_recv.at[h], tensor=other_t)

    def frozen(s):
        def rows(b, carry):
            value = product(cot[0, columns(b)], weight[s, 0], 1, 1)
            value = value + product(cot[1, columns(b)], weight[s, 1], 1, 1)
            part[s, columns(b)] = value.astype(BF16)
            return carry

        lax.fori_loop(0, blocks, rows, 0)

        @pl.when(s // 2 != t)
        def _():
            part_copy(s, s % 2).start()

    def twin_arrival(j):
        for sub in range(2):
            twin_copy(peers[j], other_g, j, sub).wait_recv()

    frozen(f)
    pass_on(1)
    twin_arrival(0)
    frozen(peers[0])
    pass_on(2)
    for i, peer in enumerate(peers):
        go(remote(
            entries_for(peer), down_ref.at[my_blocks], d_send.at[i], d_recv.at[f], fsdp=peer
        ))
    keep_down = pltpu.make_async_copy(entries_for(f), down_ref.at[my_blocks], local_sem.at[5])
    keep_down.start()


    own[4].wait()
    for i, peer in enumerate(peers):
        remote(
            first_ref.at[my_blocks], first.at[peer], a_send.at[i], a_recv.at[peer], fsdp=peer
        ).wait_recv()

    def first_block(n, carry):
        b, s = n // 4, n % 4
        first_rows[b, pl.ds(pl.multiple_of(s * portion, 16), portion)] = trade_pairs(
            first[s, b].astype(F32)
        ).astype(BF16)
        return carry

    lax.fori_loop(0, 4 * blocks, first_block, 0)

    def low_block(b, carry):
        value = product(acts[columns(b)], first_rows[b], 1, 0)
        low_part[:, :, columns(b)] = value.T.reshape(2, ADAPTER_RANK, BLOCK).astype(BF16)
        return carry

    lax.fori_loop(0, blocks, low_block, 0)
    swap = remote(low_part.at[other_a], low_got.at[0], l_send.at[0], l_recv.at[0], adapter=other_a)
    go(swap)
    swap.wait_recv()
    low_sum[...] = (low_part[a].astype(F32) + low_got[0].astype(F32)).astype(BF16)
    swap = remote(low_sum, low_got.at[1], l_send.at[1], l_recv.at[1], tensor=other_t)
    go(swap)
    swap.wait_recv()
    low[...] = (low_sum[...].astype(F32) + low_got[1].astype(F32)).astype(BF16)

    def up_block(b, carry):
        value = adapter_scale * product(low[:, columns(b)], cot[a, columns(b)], 1, 0)
        up_stage[b] = value.astype(BF16)
        return carry

    lax.fori_loop(0, blocks, up_block, 0)

    def ranks_for(device):
        return up_stage.at[:, pl.ds(pl.multiple_of(device * ranks, 16), ranks)]

    for i, peer in enumerate(peers):
        go(remote(ranks_for(peer), up_ref.at[a, my_blocks], u_send.at[i], u_recv.at[f], fsdp=peer))
    keep_up = pltpu.make_async_copy(ranks_for(f), up_ref.at[a, my_blocks], local_sem.at[6])
    keep_up.start()

    twin_arrival(1)
    frozen(peers[1])
    twin_arrival(2)
    frozen(peers[2])
    keep_up.wait()
    for i, peer in enumerate(peers):
        there = up_ref.at[a, pl.ds(peer * blocks, blocks)]
        remote(ranks_for(peer), there, u_send.at[i], u_recv.at[peer], fsdp=peer).wait_recv()
    go(remote(up_ref.at[a], up_ref.at[a], x_send.at[0], x_recv.at[0], adapter=other_a))

    for h in range(2):
        part_copy(2 * t + h, h).wait_recv()
    width = part.shape[2]

    def ig_copy(b):
        return pltpu.make_async_copy(ig.at[columns(b)], ig_ref.at[columns(b)], ig_sem.at[b])

    def final_block(b, carry):
        grad = head_of(b).astype(F32).T.astype(BF16)
        for h in range(2):
            term = product(grad, first_rows[b, pl.ds(h * width, width)], 1, 1)
            base = part[2 * t + h, columns(b)].astype(F32) + part_got[h, columns(b)].astype(F32)
            ig[columns(b), pl.ds(h * width, width)] = (base + adapter_scale * term).astype(BF16)
        ig_copy(b).start()
        return carry

    lax.fori_loop(0, blocks, final_block, 0)

    keep_down.wait()
    for i, peer in enumerate(peers):
        remote(
            entries_for(peer), down_ref.at[pl.ds(peer * blocks, blocks)],
            d_send.at[i], d_recv.at[peer], fsdp=peer,
        ).wait_recv()
    remote(up_ref.at[other_a], up_ref.at[other_a], x_send.at[0], x_recv.at[0], adapter=other_a).wait_recv()
    for h in range(2):
        part_copy(2 * other_t + h, h).wait_send()
    for copy in pending:
        copy.wait_send()
    for b in range(blocks):
        ig_copy(b).wait()

    @pl.when(inner)
    def _():
        for sub in range(2):
            weight_copy(f, sub, 1, 3 - f).wait_send()
            for j in range(3):
                weight_copy(peers[j], sub, 2 + j, onward[j]).wait_send()


def slice_on_device(
    acts,
    cotangent,
    key_value_weight,
    adapter_first_factor,
    adapter_second_factor,
    adapter_of_block,
    occupied_rows,
):
    f = lax.axis_index("fsdp")
    a = lax.axis_index("adapter")
    quarter, _, head_half = cotangent.shape
    rows, features = acts.shape
    blocks = rows // BLOCK
    all_blocks = adapter_of_block.shape[0]
    total, _, length = adapter_first_factor.shape
    ranks = adapter_second_factor.shape[2]
    portion = length // ADAPTER_RANK
    shard = key_value_weight.shape[0]
    anywhere = pl.BlockSpec(memory_space=pl.ANY)
    in_vmem = pl.BlockSpec(memory_space=pltpu.VMEM)
    in_smem = pl.BlockSpec(memory_space=pltpu.SMEM)
    dma = pltpu.SemaphoreType.DMA

    quarter_blocks = quarter // BLOCK
    live = lax.dynamic_slice_in_dim(
        occupied_rows, f * blocks + a * quarter_blocks, quarter_blocks, 0
    )
    kept = jnp.arange(BLOCK, dtype=jnp.int32)[None, :] < live[:, None]
    masked = jnp.where(
        kept[:, :, None, None],
        cotangent.reshape(quarter_blocks, BLOCK, 2, head_half),
        jnp.zeros((), BF16),
    )
    masked = masked.reshape(quarter, 2, head_half).transpose(1, 0, 2)
    weight = key_value_weight.transpose(1, 0, 2)

    first_used, second_used = pl.pallas_call(
        pick_kernel,
        out_shape=(
            jax.ShapeDtypeStruct((all_blocks, 2, length), BF16),
            jax.ShapeDtypeStruct((all_blocks, 2, ranks, head_half), BF16),
        ),
        in_specs=[in_smem, anywhere, anywhere],
        out_specs=(in_vmem, in_vmem),
        scratch_shapes=[dma((all_blocks,)), dma((all_blocks,))],
        name="pick",
    )(adapter_of_block, adapter_first_factor, adapter_second_factor)
    first_used = first_used.reshape(all_blocks, 2, length // 128, 128).transpose(0, 2, 1, 3)
    first_used = first_used.reshape(all_blocks, portion, 128)

    span = 8
    input_gradient, back_down, back_up = pl.pallas_call(
        layer_kernel,
        out_shape=(
            jax.ShapeDtypeStruct((rows, features), BF16),
            jax.ShapeDtypeStruct((all_blocks, portion, 128), BF16),
            jax.ShapeDtypeStruct((2, all_blocks, ranks, head_half), BF16),
        ),
        in_specs=[anywhere] * 5,
        out_specs=(anywhere, anywhere, anywhere),
        scratch_shapes=[
            pltpu.VMEM((2, rows, head_half), BF16),
            pltpu.VMEM((4, 2, shard, head_half), BF16),
            pltpu.VMEM((4, blocks, portion, 128), BF16),
            pltpu.VMEM((blocks, features, 128), BF16),
            pltpu.VMEM((blocks, ADAPTER_RANK, head_half), BF16),
            pltpu.VMEM((rows, features), BF16),
            pltpu.VMEM((ADAPTER_RANK, rows), BF16),
            pltpu.VMEM((ADAPTER_RANK, rows), BF16),
            pltpu.VMEM((2, ADAPTER_RANK, rows), BF16),
            pltpu.VMEM((2, ADAPTER_RANK, rows), BF16),
            pltpu.VMEM((2, ADAPTER_RANK, rows), BF16),
            pltpu.VMEM((ADAPTER_RANK, rows), BF16),
            pltpu.VMEM((ADAPTER_RANK, rows), BF16),
            pltpu.VMEM((blocks, features, 128), BF16),
            pltpu.VMEM((blocks, ADAPTER_RANK, head_half), BF16),
            pltpu.VMEM((4, rows, shard), BF16),
            pltpu.VMEM((2, rows, shard), BF16),
            pltpu.VMEM((rows, features), BF16),
            dma((7,)),
            dma((3,)), dma((4,)), dma((3,)), dma((4,)),
            dma((3,)), dma((4,)), dma((3,)), dma((4,)),
            dma((2,)), dma((2,)), dma((2,)), dma((2,)), dma((2,)), dma((2,)),
            dma((5, 2)), dma((4, 2)), dma((3, 2)), dma((4, 2)),
            dma((2,)), dma((2,)), dma((1,)), dma((1,)), dma((blocks,)),
        ],
        compiler_params=pltpu.CompilerParams(
            collective_id=0, has_side_effects=True, vmem_limit_bytes=58 * 2**20
        ),
        name="layer",
    )(masked, weight, first_used, second_used, acts)

    input_gradient, down_grad, up_grad = pl.pallas_call(
        table_kernel,
        out_shape=(
            jax.ShapeDtypeStruct((rows, features), BF16),
            jax.ShapeDtypeStruct((total, portion, 128), BF16),
            jax.ShapeDtypeStruct((total, 2, ranks, head_half), BF16),
        ),
        in_specs=[in_smem, anywhere, anywhere, anywhere],
        out_specs=(anywhere, anywhere, anywhere),
        scratch_shapes=[
            pltpu.VMEM((span, portion, 128), BF16),
            pltpu.VMEM((span, 2, ranks, head_half), BF16),
            pltpu.VMEM((all_blocks, portion, 128), BF16),
            pltpu.VMEM((2, all_blocks, ranks, head_half), BF16),
            pltpu.VMEM((rows, features), BF16),
            pltpu.VMEM((all_blocks, portion, 128), BF16),
            pltpu.VMEM((all_blocks, 2, ranks, head_half), BF16),
            pltpu.VMEM((portion, 128), F32),
            pltpu.VMEM((2, ranks, head_half), F32),
            pltpu.SMEM((all_blocks,), jnp.int32),
            dma((2,)),
            dma((2,)),
            dma((2, total // span)),
            dma((2, all_blocks)),
        ],
        compiler_params=pltpu.CompilerParams(vmem_limit_bytes=60 * 2**20),
        name="table",
    )(adapter_of_block, back_down, back_up, input_gradient)
    down_grad = down_grad.reshape(total, length // 128, 2, 128).transpose(0, 2, 1, 3)
    return (input_gradient, down_grad.reshape(total, 2, length), up_grad)


def on_slice(*args):
    sizes = tuple(lax.axis_size(name) for name in ("groups", "fsdp", "tensor", "adapter"))
    if sizes == (2, 4, 2, 2) and args[0].shape == (4 * BLOCK, 1280):
        return slice_on_device(*args)
    return general_on_device(*args)


def solution(mesh):
    in_specs = (
        P(("groups", "fsdp"), ("adapter", "tensor")),
        P(("groups", "fsdp", "adapter"), None, "tensor"),
        P(("adapter", "fsdp"), None, "tensor"),
        P(None, None, ("adapter", "tensor", "fsdp")),
        P(None, None, "fsdp", "tensor"),
        P("groups"),
        P("groups"),
    )
    out_specs = (
        P(("groups", "fsdp"), ("adapter", "tensor")),
        P("groups", None, ("adapter", "tensor", "fsdp")),
        P("groups", None, "fsdp", "tensor"),
    )
    return jax.shard_map(
        on_slice, mesh=mesh, in_specs=in_specs, out_specs=out_specs, check_vma=False
    )
```
